256 devices in a mesh: slab: 64 (over y, x_lo, z), head: 4 (over x_hi, core).
Axes of the slice: x: 4 (x_hi: 2, x_lo: 2; x = x_hi * 2 + x_lo), y: 4, z: 8, core: 2. Of those that a mesh axis runs over, the one named last changes fastest.
Arguments:
- query_rows: bfloat16 [65536, 1536], P('slab', 'head'), may hold values from -110 to 110
- key_rows: bfloat16 [65536, 1536], P('slab', 'head'), may hold values from -4 to 4
- value_rows: bfloat16 [65536, 1536], P('slab', 'head'), may hold values from -6 to 6
- far_slab: int32 [128, 48], P('slab'), may hold values from 0 to 63, all different within a row; in each aligned block of 2 rows (0 to 1, 2 to 3, ...) at most 2 rows name the same one
- far_tile: int32 [128, 48], P('slab'), may hold values from 0 to 15
- far_count: int32 [128], P('slab'), may hold values from 24 to 48
- out_weight: bfloat16 [1536, 3072], P('head'), may hold values from -8 to 8
Outputs:
- block_output: bfloat16 [65536, 3072], P('slab', 'head')
The draws below stay inside these ranges and needn't reach their ends.
Inputs may be any that keep to these rules, and one draw needn't show every extreme that they name: `far_slab`: each row lists 48 different slabs.
All inputs are finite; a program needn't handle non-finite values.
Results may differ from the reference program's by a relative error of at most 0.0057.
Values may be sent and summed in bfloat16 or wider, within the bound.
A program may use at most 128 MiB of HBM per device.

```python
import math
import jax
import jax.numpy as jnp
import numpy as np
from jax import lax

D = 3072
HEAD_DIM = 128
TOK_DEV = 1024
QT_DEV = 2
KTILE = 64
NEAR = 256
HEADS = 12
TOKENS = 65536
QTILE = 512
QTILES = 128
KT_DEV = 16
MAXFAR = 48
N_SLAB = 64


def shared_field(key):
    shape = (TOKENS, HEADS * HEAD_DIM)
    first = jnp.clip(jax.random.normal(jax.random.fold_in(key, 101), shape, jnp.float32), -4.0, 4.0)
    return first


def draw_key_rows(key, part):
    return shared_field(key).astype(jnp.bfloat16)


def draw_query_rows(key, part):
    shape = (TOKENS, HEADS * HEAD_DIM)
    key = jax.random.fold_in(key, 3)
    return jnp.clip(jax.random.normal(key, shape, jnp.float32), -4.0, 4.0).astype(jnp.bfloat16)


def set_ends(values, stream_key, low, largest):
    index_at = [jax.random.randint(jax.random.fold_in(stream_key, axis), (), 0, length) for axis, length in enumerate(values.shape)]
    widest = values.shape.index(max(values.shape))
    neighbour = index_at[:widest] + [(index_at[widest] + 1) % values.shape[widest]] + index_at[widest + 1:]
    return values.at[tuple(index_at)].set(low).at[tuple(neighbour)].set(largest)


def with_spikes(array, stream_key, source, target, shards_of, factor):
    owner, partner = [(jnp.arange(array.shape[dim]) // (array.shape[dim] // shards_of)).reshape([-1 if axis == dim else 1 for axis in range(array.ndim)]) for dim in (source, target)]
    chosen = jax.random.permutation(stream_key, shards_of)[partner]
    strong = (owner == chosen) | (owner == (partner + shards_of // 2) % shards_of)
    return jnp.where(strong, factor * array, array)


def levels(stream_key, dims, split, least, largest):
    def one(axis_at, blocks):
        draws = jax.random.uniform(jax.random.fold_in(jax.random.fold_in(stream_key, 6), axis_at), (blocks,), jnp.float32, least / len(split), largest / len(split))
        return jnp.repeat(jnp.exp(draws), dims[axis_at] // blocks).reshape((-1,) + (1,) * (len(dims) - axis_at - 1))

    level = one(*split[0])
    for cut in split[1:]:
        level = level * one(*cut)
    return level


def shared_out(rng, own, number, rows, count, top, most, lean):
    sequence = jax.random.permutation(rng, count)
    heavy_load, common = load_shares(count, rows * top, most, lean, True), load_shares(count, rows * top, most, lean, False)
    places = jnp.arange(count)

    def named(lengths, rotation):
        used = int((lengths > 0).sum())
        fixed = max(1, used // 4)
        moved = fixed + (places - fixed + rotation * (used - fixed)) % max(1, count - fixed)
        return jnp.zeros((count,), jnp.int32).at[sequence[jnp.where(places < fixed, places, moved)]].set(jnp.asarray(lengths, jnp.int32))

    lengths = jnp.where(number % 4 == 0, named(heavy_load, number // 4), named(common, number - number // 4 - 1))
    mixed = jax.random.permutation(jax.random.fold_in(own, 3), count)
    donor, taker = mixed[0:count // 2 * 2:2], mixed[1:count // 2 * 2:2]
    margin = jnp.minimum(lengths[donor] - 1, most - lengths[taker]) // 2
    margin = jnp.where((donor == sequence[0]) | (taker == sequence[0]) | (lengths[taker] == 0), 0, jnp.maximum(margin, 0))
    moved = jax.random.randint(jax.random.fold_in(own, 4), (count // 2,), 0, 1 << 20) % (margin + 1)
    lengths = lengths.at[donor].add(-moved).at[taker].add(moved)
    members = jnp.searchsorted(jnp.cumsum(lengths), jnp.arange(rows * top), side="right").astype(jnp.int32)
    table = members.reshape(top, rows).T
    table = table[jax.random.permutation(jax.random.fold_in(own, 1), rows)]
    rotation = jax.random.randint(jax.random.fold_in(own, 2), (rows, 1), 0, top)
    return jnp.take_along_axis(table, (jnp.arange(top)[None, :] + rotation) % top, axis=1)


def load_shares(number_of, total, limit, slope, full):
    weights = [(1 << 20) // math.isqrt(rank ** slope) + 1 for rank in range(1, number_of + 1)]
    largest = limit if full else min(limit, max(-(-total // number_of), total * weights[0] // sum(weights)))
    least = 1 if total - largest >= number_of - 1 else 0
    given, surplus = [largest] + [least] * (number_of - 1), total - largest - least * (number_of - 1)
    while surplus > 0:
        movable = [i for i in range(1, number_of) if given[i] < largest] or [i for i in range(1, number_of) if given[i] < limit]
        pool, remaining = sum([weights[i] for i in movable]), surplus
        for i in movable:
            extra = min(limit - given[i], max(1, remaining * weights[i] // pool), surplus)
            given[i] = given[i] + extra
            surplus = surplus - extra
    return np.array(given)


def bell_draw(own_key, shape, scale, limit, split=(), kind=jnp.bfloat16):
    array = jax.random.normal(own_key, shape, jnp.float32) * scale
    if len(split) > 0:
        array = levels(own_key, shape, split, -0.22, 0.18) * array
    return jnp.clip(array, min=-limit, max=limit).astype(kind)


def heavy_noise(rng, shape, deviation, limit, split, heavy, held_as=jnp.bfloat16):
    drawn = deviation * jax.random.normal(rng, shape, jnp.float32)
    if split:
        drawn = drawn * levels(rng, shape, split, -0.22, 0.18)
    return jnp.clip(with_spikes(drawn, jax.random.fold_in(rng, 3), *heavy), -limit, limit).astype(held_as)


def setup_inputs(seed: int = 0) -> dict:
    keys = jax.random.split(jax.random.key(seed), 8)
    query_rows = draw_query_rows(jax.random.fold_in(keys[7], 71), 0)
    key_rows = draw_key_rows(jax.random.fold_in(keys[7], 71), 0)
    value_rows = bell_draw(keys[2], (TOKENS, HEADS * HEAD_DIM), 1.0, 6.0, ((0, 64), (1, 4)))
    far_slab_keys = jax.random.split(jax.random.fold_in(keys[3], 1), QTILES // QT_DEV)
    far_slab_turns = jax.random.permutation(jax.random.fold_in(keys[3], 3), QTILES // QT_DEV)
    far_slab = jax.vmap(lambda own, number: shared_out(jax.random.fold_in(keys[3], 2), own, number, QT_DEV, N_SLAB, MAXFAR, 2, 2))(far_slab_keys, far_slab_turns).reshape((QTILES, MAXFAR))
    far_tile = set_ends(jax.random.randint(keys[4], (QTILES, MAXFAR), 0, KT_DEV), jax.random.fold_in(keys[4], 1), 0, KT_DEV - 1).astype(jnp.int32)
    far_count = set_ends(jax.random.randint(keys[5], (QTILES,), MAXFAR // 2, MAXFAR + 1), jax.random.fold_in(keys[5], 1), MAXFAR // 2, MAXFAR).astype(jnp.int32)
    out_weight = heavy_noise(keys[6], (HEADS * HEAD_DIM, D), (max(1, HEADS * HEAD_DIM // 1024)) ** -0.5, 8.0, ((0, 4),), (0, 1, 4, 2.0))
    return dict(query_rows=query_rows, key_rows=key_rows, value_rows=value_rows, far_slab=far_slab, far_tile=far_tile, far_count=far_count, out_weight=out_weight)


NEG_BIG = -1e+30

def reference(query_rows, key_rows, value_rows, far_slab, far_tile, far_count, out_weight):
    width = HEADS * HEAD_DIM
    scale = 1.0 / math.sqrt(HEAD_DIM)
    key_pad = jnp.pad(key_rows, ((NEAR, NEAR), (0, 0)))
    value_pad = jnp.pad(value_rows, ((NEAR, NEAR), (0, 0)))
    span = TOK_DEV + 2 * NEAR
    offsets = jnp.arange(span, dtype=jnp.int32)
    inside = jnp.arange(KTILE, dtype=jnp.int32)
    slots = jnp.arange(MAXFAR, dtype=jnp.int32)

    def one_tile(tile_index):
        slab_index = tile_index // QT_DEV
        start = (slab_index * TOK_DEV).astype(jnp.int32)
        queries = lax.dynamic_slice_in_dim(query_rows, (tile_index * QTILE).astype(jnp.int32), QTILE, 0)
        near_keys = lax.dynamic_slice_in_dim(key_pad, start, span, 0)
        near_values = lax.dynamic_slice_in_dim(value_pad, start, span, 0)
        position = start - NEAR + offsets
        near_ok = (position >= 0) & (position < TOKENS)
        tile_ids = far_slab[tile_index] * KT_DEV + far_tile[tile_index]
        far_index = (tile_ids[:, None] * KTILE + inside[None, :]).reshape(-1).astype(jnp.int32)
        far_keys = jnp.take(key_rows, far_index, axis=0)
        far_values = jnp.take(value_rows, far_index, axis=0)
        far_ok = jnp.repeat(slots < far_count[tile_index], KTILE)
        all_keys = jnp.concatenate([near_keys, far_keys], axis=0)
        all_values = jnp.concatenate([near_values, far_values], axis=0)
        all_ok = jnp.concatenate([near_ok, far_ok], axis=0)
        q_three = queries.astype(jnp.float32).reshape(QTILE, HEADS, HEAD_DIM)
        k_three = all_keys.astype(jnp.float32).reshape(-1, HEADS, HEAD_DIM)
        v_three = all_values.astype(jnp.float32).reshape(-1, HEADS, HEAD_DIM)
        scores = jnp.einsum('qhd,khd->hqk', q_three, k_three) * scale
        scores = jnp.where(all_ok[None, None, :], scores, NEG_BIG)
        highest = lax.optimization_barrier(jnp.max(scores, axis=2, keepdims=True))
        weights = jnp.exp(scores - highest)
        probs = (weights / lax.optimization_barrier(jnp.sum(weights, axis=2, keepdims=True))).astype(jnp.bfloat16)
        attended = jnp.einsum('hqk,khd->qhd', probs.astype(jnp.float32), v_three)
        return attended.reshape(QTILE, width).astype(jnp.bfloat16)
    tiles = lax.map(one_tile, jnp.arange(QTILES, dtype=jnp.int32))
    attended = tiles.reshape(TOKENS, width)
    return jnp.dot(attended, out_weight, preferred_element_type=jnp.float32).astype(jnp.bfloat16)
```

```python
import math

import jax
import jax.numpy as jnp
from jax import lax
from jax.experimental import pallas as pl
from jax.experimental.pallas import tpu as pltpu
from jax.sharding import PartitionSpec as P

HD = 128
KTILE = 64
NEAR = 256
TOK = 1024
KT = TOK // KTILE
NT = NEAR // KTILE
H = 3
NY, NX, NZ = 4, 2, 8
NG = NY * NX
NHEAD = 4
SLABS = NG * NZ
SLOTS = 48
QC = 256
OUTC = 768
NEG = -1e30
SCALE = math.log2(math.e) / math.sqrt(HD)
MESH = pl.DeviceIdType.MESH


def kernel(q_hbm, k_hbm, v_hbm, fs, ft, fc, w_hbm, out_ref, *scratch):
    (own, near, qv, send, recv, att, wr, oacc, mst, lst, acc, bias, nbias, reqv, reqr, reqs,
     zs, zr, ps, pr, rs, rr, hs, hr, ws, wrs, ats, atr, loc) = scratch[:29]
    zrefs = scratch[29:]
    offs = (1, 2, 3, 4, -1, -2, -3)
    zb = {(o, h): zrefs[i * H + h] for i, o in enumerate(offs) for h in range(H)}

    s = lax.axis_index("slab")
    g = lax.axis_index("head")
    z = lax.rem(s, NZ)
    x = lax.rem(lax.div(s, NZ), NX)
    y = lax.div(s, NZ * NX)
    base = s - z

    zright = base + lax.rem(z + 1, NZ)
    zleft = base + lax.rem(z + NZ - 1, NZ)
    snext = lax.rem(s + 1, SLABS)
    sprev = lax.rem(s + SLABS - 1, SLABS)
    xflip = s + NZ * (1 - 2 * x)
    gcore = g + 1 - 2 * lax.rem(g, 2)
    gx = lax.rem(g + 2, NHEAD)
    gxc = gx + 1 - 2 * lax.rem(gx, 2)

    def group_dst(d):
        return (lax.rem(y + lax.div(d, NX), NY) * NX + lax.rem(x + lax.rem(d, NX), NX)) * NZ + z

    def group_src(d):
        return lax.rem(y + NY - lax.div(d, NX), NY) * NX + lax.rem(x + lax.rem(d, NX), NX)

    def remote(src, dst, ssem, rsem, slab, head):
        return pltpu.make_async_remote_copy(
            src_ref=src, dst_ref=dst, send_sem=ssem, recv_sem=rsem,
            device_id=(slab, head), device_id_type=MESH)

    loads = []
    for h in range(H):
        cols = slice(h * HD, (h + 1) * HD)
        loads.append(pltpu.make_async_copy(k_hbm.at[:, :, cols], own.at[h, 0], loc.at[2 * h]))
        loads.append(pltpu.make_async_copy(v_hbm.at[:, :, cols], own.at[h, 1], loc.at[2 * h + 1]))
    for c in loads:
        c.start()
    qload = pltpu.make_async_copy(q_hbm, qv, loc.at[6])
    qload.start()

    barrier = pltpu.get_barrier_semaphore()

    def greet(slab, head):
        pl.semaphore_signal(barrier, inc=1, device_id=(slab, head), device_id_type=MESH)

    for slab, head in ((zright, g), (zleft, g), (snext, g), (sprev, g), (s, gcore), (s, gx),
                       (xflip, gx), (xflip, gxc)):
        greet(slab, head)

    @pl.loop(1, NG)
    def _(d):
        greet(group_dst(d), g)

    for c in loads:
        c.wait()
    pl.semaphore_wait(barrier, 8 + NG - 1)

    zcopies = {}

    def z_start(h, step):
        for kv in range(2):
            for way, sign, target in ((0, -1, zright), (1, 1, zleft)):
                if step == NZ // 2 and way != kv:
                    continue
                src = own.at[h, kv] if step == 1 else zb[sign * (step - 1), h].at[kv]
                dst = zb[NZ // 2 if step == NZ // 2 else sign * step, h].at[kv]
                c = remote(src, dst, zs.at[way, h, step - 1, kv], zr.at[way, h, step - 1, kv], target, g)
                c.start()
                zcopies[way, h, step, kv] = c

    z_start(0, 1)

    lane = lax.broadcasted_iota(jnp.int32, (SLABS, 128), 1)
    row = lax.broadcasted_iota(jnp.int32, (SLABS, 128), 0)

    def want(j, table):
        for r in range(2):
            table = jnp.where((row == fs[r, j]) & (lane == r), ft[r, j], table)
        return table

    reqv[...] = lax.fori_loop(0, SLOTS, want, jnp.zeros((SLABS, 128), jnp.int32))

    def req_copy(d):
        ring = group_src(d)
        return remote(reqv.at[pl.ds(pl.multiple_of(ring * NZ, NZ), NZ)], reqr.at[d], rs.at[d], rr.at[d],
                      ring * NZ + z, g)

    @pl.loop(1, NG)
    def _(d):
        req_copy(d).start()

    reqr[0] = reqv[pl.ds(pl.multiple_of(base, NZ), NZ), :]

    mid = pltpu.make_async_copy(own, near.at[:, :, NT:NT + KT], loc.at[7])
    mid.start()
    halo = [
        remote(own.at[:, :, KT - NT:], near.at[:, :, :NT], hs.at[0], hr.at[0], snext, g),
        remote(own.at[:, :, :NT], near.at[:, :, NT + KT:], hs.at[1], hr.at[1], sprev, g),
    ]
    for c in halo:
        c.start()

    @pl.loop(1, NG)
    def _(d):
        req_copy(d).wait_recv()

    tosm = pltpu.make_async_copy(reqr, reqs, loc.at[8])
    tosm.start()
    tosm.wait()

    def tile_copy(h, step, d):
        b = step % (NZ // 2)
        if b == 0:
            half = 0 if step == 0 else 1
            rows = slice(half * KTILE, (half + 1) * KTILE)
        else:
            rows = slice(0, 2 * KTILE)
        return remote(send.at[h, b, d, :, :, rows, :], recv.at[h, b, d, :, :, rows, :],
                      ps.at[h, step, d], pr.at[h, step, d], group_dst(d), g)

    def select(h, step):
        b = step % (NZ // 2)
        if step == 0:
            parts = ((own, 0, 0),)
        elif b == 0:
            parts = ((zb[NZ // 2, h], NZ // 2, 1),)
        else:
            parts = ((zb[step, h], step, 0), (zb[-step, h], -step, 1))

        def pick(d, dst):
            for ref, off, half in parts:
                zz = lax.rem(z + (off + NZ), NZ)
                for r in range(2):
                    tile = reqs[d, zz, r]
                    for kv in range(2):
                        got = own[h, kv, tile] if step == 0 else ref[kv, tile]
                        dst[h, b, d, kv, r, half * KTILE:(half + 1) * KTILE, :] = got

        @pl.loop(1, NG)
        def _(d):
            pick(d, send)
            tile_copy(h, step, d).start()

        pick(0, recv)

    for h in range(H):
        select(h, 0)

    def w_cols(j):
        return w_hbm.at[:, :, pl.ds(pl.multiple_of(j * OUTC, OUTC), OUTC)]

    w_rows = wr.at[:, pl.ds(pl.multiple_of(g * HD, HD), HD), :]
    wown = pltpu.make_async_copy(w_cols(g), w_rows, loc.at[9])
    wown.start()
    wcopies = [
        remote(w_cols(j), w_rows, ws.at[i], wrs.at[i], slab, j)
        for i, (slab, j) in enumerate(((s, gcore), (xflip, gx), (xflip, gxc)))
    ]
    for c in wcopies:
        c.start()

    key = lax.broadcasted_iota(jnp.int32, (8, NG * 2 * KTILE), 1)
    blk = lax.broadcasted_iota(jnp.int32, (8, NG * 2 * KTILE), 0)
    d_of = key // (2 * KTILE)
    half = (key // KTILE) % 2
    off = jnp.where(blk == 0, half * (NZ // 2), jnp.where(half == 0, blk, NZ - blk))
    ring = ((y + NY - d_of // NX) % NY) * NX + (x + d_of % NX) % NX
    slab_of = ring * NZ + (z + off) % NZ
    for r in range(2):
        count = fc[r]

        def mark(j, table):
            return jnp.where((slab_of == fs[r, j]) & (j < count), 0.0, table)

        bias[r] = lax.fori_loop(0, SLOTS, mark, jnp.full((8, NG * 2 * KTILE), NEG, jnp.float32))
    pos = lax.broadcasted_iota(jnp.int32, (1, TOK + 2 * NEAR), 1) + (s * TOK - NEAR)
    nbias[...] = jnp.where((pos >= 0) & (pos < SLABS * TOK), 0.0, NEG)

    def attend(h, i, keys, values, mask, first):
        rows = pl.ds(pl.multiple_of(i * QC, QC), QC)
        scores = lax.dot_general(qv[rows, h * HD:(h + 1) * HD], keys, (((1,), (1,)), ((), ())),
                                 preferred_element_type=jnp.float32)
        scores = scores * SCALE + mask
        top = jnp.max(scores, axis=1, keepdims=True)
        if not first:
            before = mst[rows, :1]
            top = jnp.maximum(before, top)
        weights = jnp.exp2(scores - top)
        total = jnp.sum(weights, axis=1, keepdims=True)
        mixed = jnp.dot(weights.astype(jnp.bfloat16), values, preferred_element_type=jnp.float32)
        if not first:
            fade = jnp.exp2(before - top)
            total = total + fade * lst[rows, :1]
            mixed = mixed + fade * acc[rows, :]
        return rows, top, total, mixed

    def keep(rows, top, total, mixed):
        mst[rows, :] = jnp.broadcast_to(top, (QC, 128))
        lst[rows, :] = jnp.broadcast_to(total, (QC, 128))
        acc[rows, :] = mixed

    def attend_near(h):
        if h == 0:
            qload.wait()
            mid.wait()
            for c in halo:
                c.wait_recv()

        @pl.loop(0, TOK // QC)
        def _(i):
            keep(*attend(h, i, near[h, 0].reshape(-1, HD), near[h, 1].reshape(-1, HD), nbias[...], True))

    def attend_far(h, b):
        for step in ((0, NZ // 2) if b == 0 else (b,)):
            @pl.loop(1, NG)
            def _(d):
                tile_copy(h, step, d).wait_recv()

        @pl.loop(0, TOK // QC)
        def _(i):
            r = lax.div(i, TOK // 2 // QC)
            keys = recv[h, b, :, 0, r].reshape(NG * 2 * KTILE, HD)
            values = recv[h, b, :, 1, r].reshape(NG * 2 * KTILE, HD)
            got = attend(h, i, keys, values, bias[r, b:b + 1, :], False)
            if b != 0:
                keep(*got)
            else:
                rows, _, total, mixed = got
                att[h, g, rows, :] = (mixed / total).astype(jnp.bfloat16)

    acopies = {}

    def share(h):
        for i, head in ((0, gcore), (1, gx)):
            acopies[h, i] = remote(att.at[h, g], att.at[h, g], ats.at[h, i], atr.at[h, i], s, head)
            acopies[h, i].start()

    def relay(h):
        acopies[h, 1].wait_recv()
        acopies[h, 2] = remote(att.at[h, gx], att.at[h, gx], ats.at[h, 2], atr.at[h, 2], s, gcore)
        acopies[h, 2].start()

    def project(h):
        acopies[h, 0].wait_recv()
        acopies[h, 2].wait_recv()
        if h == 0:
            wown.wait()
            for c in wcopies:
                c.wait_recv()

        @pl.loop(0, TOK // QC)
        def _(i):
            rows = pl.ds(pl.multiple_of(i * QC, QC), QC)
            left = jnp.concatenate([att[h, j, rows, :] for j in range(NHEAD)], axis=1)
            part = jnp.dot(left, wr[h], preferred_element_type=jnp.float32)
            if h > 0:
                part = part + oacc[rows, :]
            if h < H - 1:
                oacc[rows, :] = part
            else:
                out_ref[rows, :] = part.astype(jnp.bfloat16)

    items = []
    for h in range(H):
        for n, b in enumerate((1, 2, 3, 0)):
            def item(h=h, b=b, n=n):
                if n == 0:
                    attend_near(h)
                attend_far(h, b)
                if b == 0:
                    share(h)
                if h > 0 and n == 0:
                    relay(h - 1)
                if h > 0 and n == 1:
                    project(h - 1)
            items.append(item)

    LAG = 4
    done = 0
    stage = 0
    for h in range(H):
        for step in range(1, NZ // 2 + 1):
            for kv in range(2):
                for way in range(2):
                    if (way, h, step, kv) in zcopies:
                        zcopies[way, h, step, kv].wait_recv()
            if step < NZ // 2:
                z_start(h, step + 1)
            if step == NZ // 2 - 1 and h + 1 < H:
                z_start(h + 1, 1)
            select(h, step)
            stage += 1
            if stage > LAG:
                items[done]()
                done += 1
    while done < len(items):
        items[done]()
        done += 1
    relay(H - 1)
    project(H - 1)

    for c in zcopies.values():
        c.wait_send()
    for h in range(H):
        for step in range(NZ // 2 + 1):
            @pl.loop(1, NG)
            def _(d):
                tile_copy(h, step, d).wait_send()

    @pl.loop(1, NG)
    def _(d):
        req_copy(d).wait_send()

    for c in halo + wcopies + list(acopies.values()):
        c.wait_send()


def body(query_rows, key_rows, value_rows, far_slab, far_tile, far_count, out_weight):
    vm = pltpu.VMEM
    dma = pltpu.SemaphoreType.DMA
    bf = jnp.bfloat16
    f32 = jnp.float32
    any_spec = pl.BlockSpec(memory_space=pl.ANY)
    smem_spec = pl.BlockSpec(memory_space=pltpu.SMEM)
    scratch = [
        vm((H, 2, KT, KTILE, HD), bf),
        vm((H, 2, KT + 2 * NT, KTILE, HD), bf),
        vm((TOK, H * HD), bf),
        vm((H, NZ // 2, NG, 2, 2, 2 * KTILE, HD), bf),
        vm((H, NZ // 2, NG, 2, 2, 2 * KTILE, HD), bf),
        vm((H, NHEAD, TOK, HD), bf),
        vm((H, NHEAD * HD, OUTC), bf),
        vm((TOK, OUTC), f32),
        vm((TOK, 128), f32),
        vm((TOK, 128), f32),
        vm((TOK, HD), f32),
        vm((2, 8, NG * 2 * KTILE), f32),
        vm((1, TOK + 2 * NEAR), f32),
        vm((SLABS, 128), jnp.int32),
        vm((NG, NZ, 128), jnp.int32),
        pltpu.SMEM((NG, NZ, 128), jnp.int32),
        dma((2, H, NZ // 2, 2)), dma((2, H, NZ // 2, 2)),
        dma((H, NZ // 2 + 1, NG)), dma((H, NZ // 2 + 1, NG)),
        dma((NG,)), dma((NG,)),
        dma((2,)), dma((2,)),
        dma((3,)), dma((3,)),
        dma((H, 3)), dma((H, 3)),
        dma((10,)),
    ] + [vm((2, KT, KTILE, HD), bf) for _ in range((NZ - 1) * H)]
    call = pl.pallas_call(
        kernel,
        out_shape=jax.ShapeDtypeStruct((TOK, OUTC), bf),
        in_specs=[any_spec, any_spec, any_spec, smem_spec, smem_spec, smem_spec, any_spec],
        out_specs=pl.BlockSpec(memory_space=pltpu.VMEM),
        scratch_shapes=scratch,
        compiler_params=pltpu.CompilerParams(
            collective_id=0, has_side_effects=True, vmem_limit_bytes=60 * 1024 * 1024),
        cost_estimate=pl.CostEstimate(
            flops=12_000_000_000, bytes_accessed=8_000_000, transcendentals=18_000_000),
    )
    return call(query_rows, key_rows.reshape(KT, KTILE, H * HD), value_rows.reshape(KT, KTILE, H * HD), far_slab, far_tile, far_count,
                out_weight.reshape(H, HD, NHEAD * OUTC))


def solution(mesh):
    return jax.shard_map(
        body,
        mesh=mesh,
        in_specs=(
            P("slab", "head"),
            P("slab", "head"),
            P("slab", "head"),
            P("slab", None),
            P("slab", None),
            P("slab"),
            P("head", None),
        ),
        out_specs=P("slab", "head"),
        check_vma=False,
    )
```

```python
import math

import jax
import jax.numpy as jnp
from jax import lax
from jax.experimental import pallas as pl
from jax.experimental.pallas import tpu as pltpu
from jax.sharding import PartitionSpec as P

HD = 128
KTILE = 64
NEAR = 256
TOK = 1024
KT = TOK // KTILE
NT = NEAR // KTILE
H = 3
NY, NX, NZ = 4, 2, 8
NG = NY * NX
NHEAD = 4
SLABS = NG * NZ
SLOTS = 48
QC = 256
OUTC = 768
HX, KX = -1, 0
NEG = -1e30
SCALE = math.log2(math.e) / math.sqrt(HD)
MESH = pl.DeviceIdType.MESH
HALF = TOK // 2
STAGES = ((0, 1), (0, 2), (1, 1), (0, 3), (1, 2), (0, 4), (1, 3), (2, 1), (1, 4), (2, 2), (2, 3), (2, 4))
STARTS = (((0, 1), 1), ((0, 3), 2))
LAG = 5
BETWEEN = {(2, 2): ((0, 0),), (2, 3): ((1, 0), (0, 1)), (2, 4): ((1, 1),)}


def kernel(q_hbm, k_hbm, v_hbm, fs, ft, fc, fsv, ftv, w_hbm, out_ref, *scratch):
    (own, near, qv, send, recv, att, wr, oacc, mst, lst, acc, bias, nbias, pk, pkr, reqv, reqs,
     zs, zr, ps, pr, rs, rr, hs, hr, ws, wrs, ats, atr, xs, loc) = scratch[:31]
    zrefs = scratch[31:]
    offs = (1, 2, 3, 4, -1, -2, -3)
    zb = {(o, h): zrefs[i * H + h] for i, o in enumerate(offs) for h in range(H)}
    xrefs = zrefs[len(offs) * H:]
    xb = {o: xrefs[i] for i, o in enumerate((0,) + offs)}

    s = lax.axis_index("slab")
    g = lax.axis_index("head")
    z = lax.rem(s, NZ)
    x = lax.rem(lax.div(s, NZ), NX)
    y = lax.div(s, NZ * NX)
    base = s - z

    zright = base + lax.rem(z + 1, NZ)
    zleft = base + lax.rem(z + NZ - 1, NZ)
    ring_next = lax.rem(s + NZ, SLABS)
    ring_prev = lax.rem(s + SLABS - NZ, SLABS)
    xflip = s + NZ * (1 - 2 * x)
    gcore = g + 1 - 2 * lax.rem(g, 2)
    gx = lax.rem(g + 2, NHEAD)
    gxc = gx + 1 - 2 * lax.rem(gx, 2)

    def group_dst(d):
        return (lax.rem(y + lax.rem(d, NY), NY) * NX + lax.rem(x + lax.div(d, NY), NX)) * NZ + z

    def group_src(d):
        return lax.rem(y + NY - lax.rem(d, NY), NY) * NX + lax.rem(x + lax.div(d, NY), NX)

    def remote(src, dst, ssem, rsem, slab, head):
        return pltpu.make_async_remote_copy(
            src_ref=src, dst_ref=dst, send_sem=ssem, recv_sem=rsem,
            device_id=(slab, head), device_id_type=MESH)

    loads = []
    for h in range(H):
        cols = slice(h * HD, (h + 1) * HD)
        loads.append(pltpu.make_async_copy(k_hbm.at[:, :, cols], own.at[h, 0], loc.at[2 * h]))
        loads.append(pltpu.make_async_copy(v_hbm.at[:, :, cols], own.at[h, 1], loc.at[2 * h + 1]))
    for c in loads:
        c.start()
    qload = pltpu.make_async_copy(q_hbm, qv, loc.at[6])
    qload.start()

    barrier = pltpu.get_barrier_semaphore()

    def greet(slab, head):
        pl.semaphore_signal(barrier, inc=1, device_id=(slab, head), device_id_type=MESH)

    for slab, head in ((zright, g), (zleft, g), (s, gcore), (s, gx),
                       (xflip, gx), (xflip, gxc)):
        greet(slab, head)

    @pl.loop(1, NG)
    def _(d):
        greet(group_dst(d), g)

    for c in loads:
        c.wait()
    pl.semaphore_wait(barrier, 6 + NG - 1)

    zcopies = {}

    def z_start(h, step):
        for c in range(2 if h == HX else 1):
            def at(off):
                if c == 1:
                    return xb[off]
                return own.at[h] if off == 0 else zb[off, h]

            for way, sign, target in ((0, -1, zright), (1, 1, zleft)):
                src = at(sign * (step - 1))
                dst = at(NZ // 2 if step == NZ // 2 else sign * step)
                if step == NZ // 2:
                    part = slice(way * KT // 2, (way + 1) * KT // 2)
                    part = (part,) if c == 1 else (slice(0, 2), part)
                    src, dst = src.at[part], dst.at[part]
                sem = (way, h, step - 1, c)
                zcopies[sem] = remote(src, dst, zs.at[sem], zr.at[sem], target, g)
                zcopies[sem].start()

    z_start(0, 1)

    pk[...] = jnp.full((2, 8, 128), -1, jnp.int32)
    pk[0, :2, :SLOTS] = fsv[...]
    pk[1, :2, :SLOTS] = ftv[...]

    def req_copy(d):
        return remote(pk, pkr.at[d], rs.at[0], rr.at[0], group_src(d) * NZ + z, g)

    req_all = remote(pkr.at[1:], pkr.at[1:], rs.at[0], rr.at[0], s, gcore)

    @pl.loop(1, NG)
    def _(d):
        req_copy(d).start()

    pkr[0] = pk[...]

    mid = pltpu.make_async_copy(own, near.at[:, :, NT:NT + KT], loc.at[7])
    mid.start()

    def halo_up(h):
        return remote(zb[-1, h].at[:, KT - NT:], near.at[h, :, :NT], hs.at[h], hr.at[h], ring_next, g)

    def halo_down(h):
        return remote(zb[1, h].at[:, :NT], near.at[h, :, NT + KT:], hs.at[h], hr.at[h], ring_prev, g)

    def halo_start(h):
        @pl.when(z == 0)
        def _():
            halo_up(h).start()

        @pl.when(z != 0)
        def _():
            near[h, :, :NT] = zb[-1, h][:, KT - NT:]

        @pl.when(z == NZ - 1)
        def _():
            halo_down(h).start()

        @pl.when(z != NZ - 1)
        def _():
            near[h, :, NT + KT:] = zb[1, h][:, :NT]

    def halo_wait(h, sent):
        for end, copy in ((0, halo_up), (NZ - 1, halo_down)):
            @pl.when(z == end)
            def _():
                (copy(h).wait_send if sent else copy(h).wait_recv)()

    req_all.wait_recv()

    listed = pkr[:, 0]
    tiles = pkr[:, 1]
    lane = lax.broadcasted_iota(jnp.int32, (NG, 8, 128), 2)
    table = jnp.zeros((NG, 8, 128), jnp.int32)
    for n in range(2 * NZ):
        first = base if n < NZ else xflip - z
        hit = jnp.where(listed == first + n % NZ, tiles, 0)
        table = jnp.where(lane == n, jnp.sum(hit, axis=2, keepdims=True), table)
    reqv[...] = table
    tosm = pltpu.make_async_copy(reqv, reqs, loc.at[8])
    tosm.start()
    tosm.wait()

    both = slice(0, 2)
    if_plain = ((1, NG, 0, 0, both),)
    if_first = (
        (NY, NG, 0, 0, slice(1 - KX, 2 - KX)),
        (1, NY, 0, 0, both),
        (NY + 1, NG, NY, 1, slice(KX, KX + 1)),
    )

    def groups(h):
        return enumerate(if_first if h == HX else if_plain)

    def tile_refs(h, step, slot, kvs):
        b = step % (NZ // 2)
        rows = slice(0, 2 * KTILE)
        if b == 0:
            half = 0 if step == 0 else 1
            rows = slice(half * KTILE, (half + 1) * KTILE)
        return send.at[h, b, slot, kvs, :, rows, :], recv.at[h, b, slot, kvs, :, rows, :]

    def tile_copy(h, step, n, slot, d, kvs):
        return remote(*tile_refs(h, step, slot, kvs), ps.at[h, step, n], pr.at[h, step, n], group_dst(d), g)

    def tile_all(h, step):
        return [remote(*tile_refs(h, step, slice(lo, hi), kvs), ps.at[h, step, n], pr.at[h, step, n], s, gcore)
                for n, (lo, hi, _, _, kvs) in groups(h)]

    def pick(h, step, slot, d, other, kvs, dst):
        b = step % (NZ // 2)
        for half, off in ((0, 0),) if step == 0 else (((1, step),) if b == 0 else ((0, step), (1, -step))):
            lane_of = lax.rem(z + (off + NZ), NZ) + NZ * other
            for r in range(2):
                tile = reqs[d, r, lane_of]
                for kv in range(kvs.start, kvs.stop):
                    if other:
                        got = xb[off][tile]
                    else:
                        got = own[h, kv, tile] if off == 0 else zb[off, h][kv, tile]
                    dst[h, b, slot, kv, r, half * KTILE:(half + 1) * KTILE, :] = got

    def select(h, step):
        for n, (lo, hi, back, other, kvs) in groups(h):
            @pl.loop(lo, hi)
            def _(slot):
                pick(h, step, slot, slot - back, other, kvs, send)
                tile_copy(h, step, n, slot, slot - back, kvs).start()

        pick(h, step, 0, 0, 0, both, recv)
        if h == HX:
            pick(h, step, NY, 0, 1, slice(KX, KX + 1), recv)

    for h in range(H):
        select(h, 0)

    def w_cols(j):
        return w_hbm.at[:, :, pl.ds(pl.multiple_of(j * OUTC, OUTC), OUTC)]

    w_rows = wr.at[:, pl.ds(pl.multiple_of(g * HD, HD), HD), :]
    wown = pltpu.make_async_copy(w_cols(g), w_rows, loc.at[9])
    wown.start()
    wcopies = [
        remote(w_cols(j), w_rows, ws.at[i], wrs.at[i], slab, j)
        for i, (slab, j) in enumerate(((s, gcore), (xflip, gx), (xflip, gxc)))
    ]
    for c in wcopies:
        c.start()

    key = lax.broadcasted_iota(jnp.int32, (8, NG * 2 * KTILE), 1)
    blk = lax.broadcasted_iota(jnp.int32, (8, NG * 2 * KTILE), 0)
    d_of = jnp.where(blk == 0, (key // KTILE) % NG, key // (2 * KTILE))
    half = jnp.where(blk == 0, key // (NG * KTILE), (key // KTILE) % 2)
    off = jnp.where(blk == 0, half * (NZ // 2), jnp.where(half == 0, blk, NZ - blk))
    ring = ((y + NY - d_of % NY) % NY) * NX + (x + d_of // NY) % NX
    slab_of = ring * NZ + (z + off) % NZ
    for r in range(2):
        count = fc[r]

        def mark(j, table):
            return jnp.where((slab_of == fs[r, j]) & (j < count), 0.0, table)

        bias[r] = lax.fori_loop(0, SLOTS, mark, jnp.full((8, NG * 2 * KTILE), NEG, jnp.float32))
    pos = lax.broadcasted_iota(jnp.int32, (1, TOK + 2 * NEAR), 1) + (s * TOK - NEAR)
    nbias[...] = jnp.where((pos >= 0) & (pos < SLABS * TOK), 0.0, NEG)

    def attend(h, i, keys, values, mask, first):
        rows = pl.ds(pl.multiple_of(i * QC, QC), QC)
        scores = lax.dot_general(qv[rows, h * HD:(h + 1) * HD], keys, (((1,), (1,)), ((), ())),
                                 preferred_element_type=jnp.float32)
        scores = scores * SCALE + mask
        top = jnp.max(scores, axis=1, keepdims=True)
        if not first:
            before = mst[rows, :1]
            top = jnp.maximum(before, top)
        weights = jnp.exp2(scores - top)
        total = jnp.sum(weights, axis=1, keepdims=True)
        mixed = jnp.dot(weights.astype(jnp.bfloat16), values, preferred_element_type=jnp.float32)
        if not first:
            fade = jnp.exp2(before - top)
            total = total + fade * lst[rows, :1]
            mixed = mixed + fade * acc[rows, :]
        return rows, top, total, mixed

    def keep(rows, top, total, mixed):
        mst[rows, :] = jnp.broadcast_to(top, (QC, 128))
        lst[rows, :] = jnp.broadcast_to(total, (QC, 128))
        acc[rows, :] = mixed

    def attend_near(h):
        if h == 0:
            qload.wait()
            mid.wait()
        halo_wait(h, False)

        @pl.loop(0, TOK // QC)
        def _(i):
            keep(*attend(h, i, near[h, 0].reshape(-1, HD), near[h, 1].reshape(-1, HD), nbias[...], True))

    def attend_far(h, step):
        b = step % (NZ // 2)
        for c in tile_all(h, step):
            c.wait_recv()
        half = 0 if step == 0 else 1
        rows = slice(0, 2 * KTILE) if b != 0 else slice(half * KTILE, (half + 1) * KTILE)
        lanes = slice(0, NG * 2 * KTILE) if b != 0 else slice(half * NG * KTILE, (half + 1) * NG * KTILE)

        for part in range(2):
            @pl.loop(part * HALF // QC, (part + 1) * HALF // QC)
            def _(i):
                keys = recv[h, b, :, 0, part, rows].reshape(-1, HD)
                values = recv[h, b, :, 1, part, rows].reshape(-1, HD)
                got = attend(h, i, keys, values, bias[part, b:b + 1, lanes], False)
                if step != NZ // 2:
                    keep(*got)
                else:
                    rows_of, _, total, mixed = got
                    att[h, g, rows_of, :] = (mixed / total).astype(jnp.bfloat16)

            if step == NZ // 2:
                share(h, part)

    acopies = {}

    def att_copy(h, part, i, which, head):
        ref = att.at[h, which, part * HALF:(part + 1) * HALF]
        acopies[h, part, i] = remote(ref, ref, ats.at[h, part, i], atr.at[h, part, i], s, head)
        acopies[h, part, i].start()

    def share(h, part):
        att_copy(h, part, 1, g, gx)
        att_copy(h, part, 0, g, gcore)

    def relay(h, part):
        acopies[h, part, 1].wait_recv()
        att_copy(h, part, 2, gx, gcore)

    def project(h, part):
        acopies[h, part, 0].wait_recv()
        acopies[h, part, 2].wait_recv()
        if h == 0 and part == 0:
            wown.wait()
            for c in wcopies:
                c.wait_recv()

        @pl.loop(part * HALF // QC, (part + 1) * HALF // QC)
        def _(i):
            rows = pl.ds(pl.multiple_of(i * QC, QC), QC)
            left = jnp.concatenate([att[h, j, rows, :] for j in range(NHEAD)], axis=1)
            piece = jnp.dot(left, wr[h], preferred_element_type=jnp.float32)
            if h > 0:
                piece = piece + oacc[rows, :]
            if h < H - 1:
                oacc[rows, :] = piece
            else:
                out_ref[rows, :] = piece.astype(jnp.bfloat16)

    items = []
    for h in range(H):
        for step in range(1, NZ // 2 + 1):
            def item(h=h, step=step):
                for what, of in BETWEEN.get((h, step), ()):
                    for part in range(2):
                        (relay if what == 0 else project)(of, part)
                if step == 1:
                    attend_near(h)
                    attend_far(h, 0)
                attend_far(h, step)
            items.append(item)

    done = 0
    for n, (h, step) in enumerate(STAGES):
        for sem, c in zcopies.items():
            if sem[1:3] == (h, step - 1):
                c.wait_recv()
        if step == 1:
            halo_start(h)
        if step < NZ // 2:
            z_start(h, step + 1)
        for then, what in STARTS:
            if then == (h, step):
                z_start(what, 1)
        select(h, step)
        if n >= LAG:
            items[done]()
            done += 1
    while done < len(items):
        items[done]()
        done += 1
    for part in range(2):
        relay(H - 1, part)
    for part in range(2):
        project(H - 1, part)

    for c in zcopies.values():
        c.wait_send()
    for h in range(H):
        for step in range(NZ // 2 + 1):
            for c in tile_all(h, step):
                c.wait_send()
        halo_wait(h, True)

    req_all.wait_send()

    for c in wcopies + list(acopies.values()):
        c.wait_send()


def body(query_rows, key_rows, value_rows, far_slab, far_tile, far_count, out_weight):
    vm = pltpu.VMEM
    dma = pltpu.SemaphoreType.DMA
    bf = jnp.bfloat16
    f32 = jnp.float32
    any_spec = pl.BlockSpec(memory_space=pl.ANY)
    smem_spec = pl.BlockSpec(memory_space=pltpu.SMEM)
    scratch = [
        vm((H, 2, KT, KTILE, HD), bf),
        vm((H, 2, KT + 2 * NT, KTILE, HD), bf),
        vm((TOK, H * HD), bf),
        vm((H, NZ // 2, NG, 2, 2, 2 * KTILE, HD), bf),
        vm((H, NZ // 2, NG, 2, 2, 2 * KTILE, HD), bf),
        vm((H, NHEAD, TOK, HD), bf),
        vm((H, NHEAD * HD, OUTC), bf),
        vm((TOK, OUTC), f32),
        vm((TOK, 128), f32),
        vm((TOK, 128), f32),
        vm((TOK, HD), f32),
        vm((2, 8, NG * 2 * KTILE), f32),
        vm((1, TOK + 2 * NEAR), f32),
        vm((2, 8, 128), jnp.int32),
        vm((NG, 2, 8, 128), jnp.int32),
        vm((NG, 8, 128), jnp.int32),
        pltpu.SMEM((NG, 8, 128), jnp.int32),
        dma((2, H, NZ // 2, 2)), dma((2, H, NZ // 2, 2)),
        dma((H, NZ // 2 + 1, 3)), dma((H, NZ // 2 + 1, 3)),
        dma((1,)), dma((1,)),
        dma((H,)), dma((H,)),
        dma((3,)), dma((3,)),
        dma((H, 2, 3)), dma((H, 2, 3)),
        dma((2,)),
        dma((10,)),
    ] + [vm((2, KT, KTILE, HD), bf) for _ in range((NZ - 1) * H)]
    scratch += [vm((KT, KTILE, HD), bf) for _ in range(NZ)]
    vmem_spec = pl.BlockSpec(memory_space=pltpu.VMEM)
    call = pl.pallas_call(
        kernel,
        out_shape=jax.ShapeDtypeStruct((TOK, OUTC), bf),
        in_specs=[any_spec, any_spec, any_spec, smem_spec, smem_spec, smem_spec, vmem_spec, vmem_spec, any_spec],
        out_specs=vmem_spec,
        scratch_shapes=scratch,
        compiler_params=pltpu.CompilerParams(
            collective_id=0, has_side_effects=True, vmem_limit_bytes=60 * 1024 * 1024),
        cost_estimate=pl.CostEstimate(
            flops=12_000_000_000, bytes_accessed=8_000_000, transcendentals=18_000_000),
    )
    return call(query_rows, key_rows.reshape(KT, KTILE, H * HD), value_rows.reshape(KT, KTILE, H * HD), far_slab, far_tile, far_count,
                far_slab, far_tile,
                out_weight.reshape(H, HD, NHEAD * OUTC))


def solution(mesh):
    return jax.shard_map(
        body,
        mesh=mesh,
        in_specs=(
            P("slab", "head"),
            P("slab", "head"),
            P("slab", "head"),
            P("slab", None),
            P("slab", None),
            P("slab"),
            P("head", None),
        ),
        out_specs=P("slab", "head"),
        check_vma=False,
    )
```

```python
import math

import jax
import jax.numpy as jnp
from jax import lax
from jax.experimental import pallas as pl
from jax.experimental.pallas import tpu as pltpu
from jax.sharding import PartitionSpec as P

HD = 128
KTILE = 64
NEAR = 256
TOK = 1024
KT = TOK // KTILE
NT = NEAR // KTILE
H = 3
NY, NX, NZ = 4, 2, 8
NG = NY * NX
NHEAD = 4
SLABS = NG * NZ
SLOTS = 48
QC = 256
OUTC = 768
HX, KX = 2, 0
NEG = -1e30
SCALE = math.log2(math.e) / math.sqrt(HD)
MESH = pl.DeviceIdType.MESH
HALF = TOK // 2
STAGES = ((0, 1), (0, 2), (1, 1), (0, 3), (1, 2), (0, 4), (1, 3), (2, 1), (1, 4), (2, 2), (3, 1), (2, 3), (3, 2),
          (2, 4), (3, 3), (3, 4))
STARTS = (((0, 1), 1), ((0, 3), 2), ((1, 4), 3))
LAG = 6
BETWEEN = {(2, 2): ((0, 0),), (2, 3): ((1, 0), (0, 1)), (2, 4): ((1, 1),)}


def kernel(q_hbm, k_hbm, v_hbm, fs, ft, fc, fsv, ftv, w_hbm, out_ref, *scratch):
    (own, near, qv, send, recv, att, wr, oacc, mst, lst, acc, bias, nbias, pk, pkr, reqv, reqs,
     zs, zr, ps, pr, rs, rr, hs, hr, ws, wrs, ats, atr, xs, loc) = scratch[:31]
    zrefs = scratch[31:]
    offs = (1, 2, 3, 4, -1, -2, -3)
    zb = {(o, h): zrefs[i * H + h] for i, o in enumerate(offs) for h in range(H)}
    xrefs = zrefs[len(offs) * H:]
    xb = {o: xrefs[i] for i, o in enumerate((0,) + offs)}

    s = lax.axis_index("slab")
    g = lax.axis_index("head")
    z = lax.rem(s, NZ)
    x = lax.rem(lax.div(s, NZ), NX)
    y = lax.div(s, NZ * NX)
    base = s - z

    zright = base + lax.rem(z + 1, NZ)
    zleft = base + lax.rem(z + NZ - 1, NZ)
    ring_next = lax.rem(s + NZ, SLABS)
    ring_prev = lax.rem(s + SLABS - NZ, SLABS)
    xflip = s + NZ * (1 - 2 * x)
    gcore = g + 1 - 2 * lax.rem(g, 2)
    gx = lax.rem(g + 2, NHEAD)
    gxc = gx + 1 - 2 * lax.rem(gx, 2)

    def group_dst(d):
        return (lax.rem(y + lax.rem(d, NY), NY) * NX + lax.rem(x + lax.div(d, NY), NX)) * NZ + z

    def group_src(d):
        return lax.rem(y + NY - lax.rem(d, NY), NY) * NX + lax.rem(x + lax.div(d, NY), NX)

    def remote(src, dst, ssem, rsem, slab, head):
        return pltpu.make_async_remote_copy(
            src_ref=src, dst_ref=dst, send_sem=ssem, recv_sem=rsem,
            device_id=(slab, head), device_id_type=MESH)

    loads = []
    for h in range(H):
        cols = slice(h * HD, (h + 1) * HD)
        loads.append(pltpu.make_async_copy(k_hbm.at[:, :, cols], own.at[h, 0], loc.at[2 * h]))
        loads.append(pltpu.make_async_copy(v_hbm.at[:, :, cols], own.at[h, 1], loc.at[2 * h + 1]))
    for c in loads:
        c.start()
    qload = pltpu.make_async_copy(q_hbm, qv, loc.at[6])
    qload.start()

    barrier = pltpu.get_barrier_semaphore()

    def greet(slab, head):
        pl.semaphore_signal(barrier, inc=1, device_id=(slab, head), device_id_type=MESH)

    for slab, head in ((zright, g), (zleft, g), (s, gcore), (s, gx),
                       (xflip, gx), (xflip, gxc)):
        greet(slab, head)

    @pl.loop(1, NG)
    def _(d):
        greet(group_dst(d), g)

    for c in loads:
        c.wait()
    pl.semaphore_wait(barrier, 6 + NG - 1)

    zcopies = {}

    def z_start(h, step):
        def at(off):
            if h == H:
                return xb[off]
            return own.at[h] if off == 0 else zb[off, h]

        for way, sign, target in ((0, -1, zright), (1, 1, zleft)):
            src = at(sign * (step - 1))
            dst = at(NZ // 2 if step == NZ // 2 else sign * step)
            if step == NZ // 2:
                part = slice(way * KT // 2, (way + 1) * KT // 2)
                part = (part,) if h == H else (slice(0, 2), part)
                src, dst = src.at[part], dst.at[part]
            sem = (way, h, step - 1)
            zcopies[sem] = remote(src, dst, zs.at[sem], zr.at[sem], target, g)
            zcopies[sem].start()

    z_start(0, 1)
    xcopy = remote(own.at[HX, KX], xb[0], xs.at[0], xs.at[1], xflip, g)
    xcopy.start()

    pk[...] = jnp.full((2, 8, 128), -1, jnp.int32)
    pk[0, :2, :SLOTS] = fsv[...]
    pk[1, :2, :SLOTS] = ftv[...]

    def req_copy(d):
        return remote(pk, pkr.at[d], rs.at[0], rr.at[0], group_src(d) * NZ + z, g)

    req_all = remote(pkr.at[1:], pkr.at[1:], rs.at[0], rr.at[0], s, gcore)

    @pl.loop(1, NG)
    def _(d):
        req_copy(d).start()

    pkr[0] = pk[...]

    mid = pltpu.make_async_copy(own, near.at[:, :, NT:NT + KT], loc.at[7])
    mid.start()

    def halo_up(h):
        return remote(zb[-1, h].at[:, KT - NT:], near.at[h, :, :NT], hs.at[h], hr.at[h], ring_next, g)

    def halo_down(h):
        return remote(zb[1, h].at[:, :NT], near.at[h, :, NT + KT:], hs.at[h], hr.at[h], ring_prev, g)

    def halo_start(h):
        @pl.when(z == 0)
        def _():
            halo_up(h).start()

        @pl.when(z != 0)
        def _():
            near[h, :, :NT] = zb[-1, h][:, KT - NT:]

        @pl.when(z == NZ - 1)
        def _():
            halo_down(h).start()

        @pl.when(z != NZ - 1)
        def _():
            near[h, :, NT + KT:] = zb[1, h][:, :NT]

    def halo_wait(h, sent):
        for end, copy in ((0, halo_up), (NZ - 1, halo_down)):
            @pl.when(z == end)
            def _():
                (copy(h).wait_send if sent else copy(h).wait_recv)()

    req_all.wait_recv()

    listed = pkr[:, 0]
    tiles = pkr[:, 1]
    lane = lax.broadcasted_iota(jnp.int32, (NG, 8, 128), 2)
    table = jnp.zeros((NG, 8, 128), jnp.int32)
    for n in range(2 * NZ):
        first = base if n < NZ else xflip - z
        hit = jnp.where(listed == first + n % NZ, tiles, 0)
        table = jnp.where(lane == n, jnp.sum(hit, axis=2, keepdims=True), table)
    reqv[...] = table
    tosm = pltpu.make_async_copy(reqv, reqs, loc.at[8])
    tosm.start()
    tosm.wait()

    both = slice(0, 2)
    if_plain = ((1, NG, 0, 0, both),)
    if_first = (
        (NY, NG, 0, 0, slice(1 - KX, 2 - KX)),
        (1, NY, 0, 0, both),
        (NY + 1, NG, NY, 1, slice(KX, KX + 1)),
    )

    def groups(h):
        return enumerate(if_first if h == HX else if_plain)

    def tile_refs(h, step, slot, kvs):
        b = step % (NZ // 2)
        rows = slice(0, 2 * KTILE)
        if b == 0:
            half = 0 if step == 0 else 1
            rows = slice(half * KTILE, (half + 1) * KTILE)
        return send.at[h, b, slot, kvs, :, rows, :], recv.at[h, b, slot, kvs, :, rows, :]

    def tile_copy(h, step, n, slot, d, kvs):
        return remote(*tile_refs(h, step, slot, kvs), ps.at[h, step, n], pr.at[h, step, n], group_dst(d), g)

    def tile_all(h, step):
        return [remote(*tile_refs(h, step, slice(lo, hi), kvs), ps.at[h, step, n], pr.at[h, step, n], s, gcore)
                for n, (lo, hi, _, _, kvs) in groups(h)]

    def pick(h, step, slot, d, other, kvs, dst):
        b = step % (NZ // 2)
        for half, off in ((0, 0),) if step == 0 else (((1, step),) if b == 0 else ((0, step), (1, -step))):
            lane_of = lax.rem(z + (off + NZ), NZ) + NZ * other
            for r in range(2):
                tile = reqs[d, r, lane_of]
                for kv in range(kvs.start, kvs.stop):
                    if other:
                        got = xb[off][tile]
                    else:
                        got = own[h, kv, tile] if off == 0 else zb[off, h][kv, tile]
                    dst[h, b, slot, kv, r, half * KTILE:(half + 1) * KTILE, :] = got

    def select(h, step):
        here = HX if h == H else h
        for n, (lo, hi, back, other, kvs) in groups(here):
            if other != (h == H):
                continue

            @pl.loop(lo, hi)
            def _(slot):
                pick(here, step, slot, slot - back, other, kvs, send)
                tile_copy(here, step, n, slot, slot - back, kvs).start()

        if h == H:
            pick(HX, step, NY, 0, 1, slice(KX, KX + 1), recv)
        else:
            pick(h, step, 0, 0, 0, both, recv)

    for h in range(H):
        select(h, 0)
    xcopy.wait_recv()
    select(H, 0)

    def w_cols(j):
        return w_hbm.at[:, :, pl.ds(pl.multiple_of(j * OUTC, OUTC), OUTC)]

    w_rows = wr.at[:, pl.ds(pl.multiple_of(g * HD, HD), HD), :]
    wown = pltpu.make_async_copy(w_cols(g), w_rows, loc.at[9])
    wown.start()
    wcopies = [
        remote(w_cols(j), w_rows, ws.at[i], wrs.at[i], slab, j)
        for i, (slab, j) in enumerate(((s, gcore), (xflip, gx), (xflip, gxc)))
    ]
    for c in wcopies:
        c.start()

    key = lax.broadcasted_iota(jnp.int32, (8, NG * 2 * KTILE), 1)
    blk = lax.broadcasted_iota(jnp.int32, (8, NG * 2 * KTILE), 0)
    d_of = jnp.where(blk == 0, (key // KTILE) % NG, key // (2 * KTILE))
    half = jnp.where(blk == 0, key // (NG * KTILE), (key // KTILE) % 2)
    off = jnp.where(blk == 0, half * (NZ // 2), jnp.where(half == 0, blk, NZ - blk))
    ring = ((y + NY - d_of % NY) % NY) * NX + (x + d_of // NY) % NX
    slab_of = ring * NZ + (z + off) % NZ
    for r in range(2):
        count = fc[r]

        def mark(j, table):
            return jnp.where((slab_of == fs[r, j]) & (j < count), 0.0, table)

        bias[r] = lax.fori_loop(0, SLOTS, mark, jnp.full((8, NG * 2 * KTILE), NEG, jnp.float32))
    pos = lax.broadcasted_iota(jnp.int32, (1, TOK + 2 * NEAR), 1) + (s * TOK - NEAR)
    nbias[...] = jnp.where((pos >= 0) & (pos < SLABS * TOK), 0.0, NEG)

    def attend(h, i, keys, values, mask, first):
        rows = pl.ds(pl.multiple_of(i * QC, QC), QC)
        scores = lax.dot_general(qv[rows, h * HD:(h + 1) * HD], keys, (((1,), (1,)), ((), ())),
                                 preferred_element_type=jnp.float32)
        scores = scores * SCALE + mask
        top = jnp.max(scores, axis=1, keepdims=True)
        if not first:
            before = mst[rows, :1]
            top = jnp.maximum(before, top)
        weights = jnp.exp2(scores - top)
        total = jnp.sum(weights, axis=1, keepdims=True)
        mixed = jnp.dot(weights.astype(jnp.bfloat16), values, preferred_element_type=jnp.float32)
        if not first:
            fade = jnp.exp2(before - top)
            total = total + fade * lst[rows, :1]
            mixed = mixed + fade * acc[rows, :]
        return rows, top, total, mixed

    def keep(rows, top, total, mixed):
        mst[rows, :] = jnp.broadcast_to(top, (QC, 128))
        lst[rows, :] = jnp.broadcast_to(total, (QC, 128))
        acc[rows, :] = mixed

    def attend_near(h):
        if h == 0:
            qload.wait()
            mid.wait()
        halo_wait(h, False)

        @pl.loop(0, TOK // QC)
        def _(i):
            keep(*attend(h, i, near[h, 0].reshape(-1, HD), near[h, 1].reshape(-1, HD), nbias[...], True))

    def attend_far(h, step):
        b = step % (NZ // 2)
        for c in tile_all(h, step):
            c.wait_recv()
        half = 0 if step == 0 else 1
        rows = slice(0, 2 * KTILE) if b != 0 else slice(half * KTILE, (half + 1) * KTILE)
        lanes = slice(0, NG * 2 * KTILE) if b != 0 else slice(half * NG * KTILE, (half + 1) * NG * KTILE)

        for part in range(2):
            @pl.loop(part * HALF // QC, (part + 1) * HALF // QC)
            def _(i):
                keys = recv[h, b, :, 0, part, rows].reshape(-1, HD)
                values = recv[h, b, :, 1, part, rows].reshape(-1, HD)
                got = attend(h, i, keys, values, bias[part, b:b + 1, lanes], False)
                if step != NZ // 2:
                    keep(*got)
                else:
                    rows_of, _, total, mixed = got
                    att[h, g, rows_of, :] = (mixed / total).astype(jnp.bfloat16)

            if step == NZ // 2:
                share(h, part)

    acopies = {}

    def att_copy(h, part, i, which, head):
        ref = att.at[h, which, part * HALF:(part + 1) * HALF]
        acopies[h, part, i] = remote(ref, ref, ats.at[h, part, i], atr.at[h, part, i], s, head)
        acopies[h, part, i].start()

    def share(h, part):
        att_copy(h, part, 1, g, gx)
        att_copy(h, part, 0, g, gcore)

    def relay(h, part):
        acopies[h, part, 1].wait_recv()
        att_copy(h, part, 2, gx, gcore)

    def project(h, part):
        acopies[h, part, 0].wait_recv()
        acopies[h, part, 2].wait_recv()
        if h == 0 and part == 0:
            wown.wait()
            for c in wcopies:
                c.wait_recv()

        @pl.loop(part * HALF // QC, (part + 1) * HALF // QC)
        def _(i):
            rows = pl.ds(pl.multiple_of(i * QC, QC), QC)
            left = jnp.concatenate([att[h, j, rows, :] for j in range(NHEAD)], axis=1)
            piece = jnp.dot(left, wr[h], preferred_element_type=jnp.float32)
            if h > 0:
                piece = piece + oacc[rows, :]
            if h < H - 1:
                oacc[rows, :] = piece
            else:
                out_ref[rows, :] = piece.astype(jnp.bfloat16)

    items = []
    for h in range(H):
        for step in range(1, NZ // 2 + 1):
            def item(h=h, step=step):
                for what, of in BETWEEN.get((h, step), ()):
                    for part in range(2):
                        (relay if what == 0 else project)(of, part)
                if step == 1:
                    attend_near(h)
                    attend_far(h, 0)
                attend_far(h, step)
            items.append(item)

    done = 0
    for n, (h, step) in enumerate(STAGES):
        for sem, c in zcopies.items():
            if sem[1:3] == (h, step - 1):
                c.wait_recv()
        if step == 1 and h < H:
            halo_start(h)
        if step < NZ // 2:
            z_start(h, step + 1)
        for then, what in STARTS:
            if then == (h, step):
                z_start(what, 1)
        select(h, step)
        if n >= LAG:
            items[done]()
            done += 1
    while done < len(items):
        items[done]()
        done += 1
    for part in range(2):
        relay(H - 1, part)
    for part in range(2):
        project(H - 1, part)

    xcopy.wait_send()
    for c in zcopies.values():
        c.wait_send()
    for h in range(H):
        for step in range(NZ // 2 + 1):
            for c in tile_all(h, step):
                c.wait_send()
        halo_wait(h, True)

    req_all.wait_send()

    for c in wcopies + list(acopies.values()):
        c.wait_send()


def body(query_rows, key_rows, value_rows, far_slab, far_tile, far_count, out_weight):
    vm = pltpu.VMEM
    dma = pltpu.SemaphoreType.DMA
    bf = jnp.bfloat16
    f32 = jnp.float32
    any_spec = pl.BlockSpec(memory_space=pl.ANY)
    smem_spec = pl.BlockSpec(memory_space=pltpu.SMEM)
    scratch = [
        vm((H, 2, KT, KTILE, HD), bf),
        vm((H, 2, KT + 2 * NT, KTILE, HD), bf),
        vm((TOK, H * HD), bf),
        vm((H, NZ // 2, NG, 2, 2, 2 * KTILE, HD), bf),
        vm((H, NZ // 2, NG, 2, 2, 2 * KTILE, HD), bf),
        vm((H, NHEAD, TOK, HD), bf),
        vm((H, NHEAD * HD, OUTC), bf),
        vm((TOK, OUTC), f32),
        vm((TOK, 128), f32),
        vm((TOK, 128), f32),
        vm((TOK, HD), f32),
        vm((2, 8, NG * 2 * KTILE), f32),
        vm((1, TOK + 2 * NEAR), f32),
        vm((2, 8, 128), jnp.int32),
        vm((NG, 2, 8, 128), jnp.int32),
        vm((NG, 8, 128), jnp.int32),
        pltpu.SMEM((NG, 8, 128), jnp.int32),
        dma((2, H + 1, NZ // 2)), dma((2, H + 1, NZ // 2)),
        dma((H, NZ // 2 + 1, 3)), dma((H, NZ // 2 + 1, 3)),
        dma((1,)), dma((1,)),
        dma((H,)), dma((H,)),
        dma((3,)), dma((3,)),
        dma((H, 2, 3)), dma((H, 2, 3)),
        dma((2,)),
        dma((10,)),
    ] + [vm((2, KT, KTILE, HD), bf) for _ in range((NZ - 1) * H)]
    scratch += [vm((KT, KTILE, HD), bf) for _ in range(NZ)]
    vmem_spec = pl.BlockSpec(memory_space=pltpu.VMEM)
    call = pl.pallas_call(
        kernel,
        out_shape=jax.ShapeDtypeStruct((TOK, OUTC), bf),
        in_specs=[any_spec, any_spec, any_spec, smem_spec, smem_spec, smem_spec, vmem_spec, vmem_spec, any_spec],
        out_specs=vmem_spec,
        scratch_shapes=scratch,
        compiler_params=pltpu.CompilerParams(
            collective_id=0, has_side_effects=True, vmem_limit_bytes=60 * 1024 * 1024),
        cost_estimate=pl.CostEstimate(
            flops=12_000_000_000, bytes_accessed=8_000_000, transcendentals=18_000_000),
    )
    return call(query_rows, key_rows.reshape(KT, KTILE, H * HD), value_rows.reshape(KT, KTILE, H * HD), far_slab, far_tile, far_count,
                far_slab, far_tile,
                out_weight.reshape(H, HD, NHEAD * OUTC))


def solution(mesh):
    return jax.shard_map(
        body,
        mesh=mesh,
        in_specs=(
            P("slab", "head"),
            P("slab", "head"),
            P("slab", "head"),
            P("slab", None),
            P("slab", None),
            P("slab"),
            P("head", None),
        ),
        out_specs=P("slab", "head"),
        check_vma=False,
    )
```

```python
import math

import jax
import jax.numpy as jnp
from jax import lax
from jax.experimental import pallas as pl
from jax.experimental.pallas import tpu as pltpu
from jax.sharding import PartitionSpec as P

HD = 128
KTILE = 64
NEAR = 256
TOK = 1024
KT = TOK // KTILE
NT = NEAR // KTILE
H = 3
NY, NX, NZ = 4, 2, 8
NG = NY * NX
NHEAD = 4
SLABS = NG * NZ
SLOTS = 48
QC = 256
OUTC = 768
HX, KX = 2, 0
NEG = -1e30
SCALE = math.log2(math.e) / math.sqrt(HD)
MESH = pl.DeviceIdType.MESH
HALF = TOK // 2
STAGES = ((0, 1), (0, 2), (1, 1), (0, 3), (1, 2), (0, 4), (1, 3), (2, 1), (1, 4), (2, 2), (3, 1), (2, 3), (3, 2),
          (2, 4), (3, 3), (3, 4))
STARTS = (((0, 1), 1), ((0, 3), 2), ((1, 4), 3))
LAG = 6
NEAR_AT = (4, 8, 11)
BETWEEN = {(2, 2): ((0, 0),), (2, 3): ((1, 0), (0, 1)), (2, 4): ((1, 1),)}


def kernel(q_hbm, k_hbm, v_hbm, fs, ft, fc, fsv, ftv, w_hbm, out_ref, *scratch):
    (own, near, qv, send, recv, att, wr, oacc, mst, lst, acc, bias, nbias, pk, pkr, reqv, reqs,
     zs, zr, ps, pr, rs, rr, hs, hr, ws, wrs, ats, atr, xs, loc) = scratch[:31]
    zrefs = scratch[31:]
    offs = (1, 2, 3, 4, -1, -2, -3)
    zb = {(o, h): zrefs[i * H + h] for i, o in enumerate(offs) for h in range(H)}
    xrefs = zrefs[len(offs) * H:]
    xb = {o: xrefs[i] for i, o in enumerate((0,) + offs)}

    s = lax.axis_index("slab")
    g = lax.axis_index("head")
    z = lax.rem(s, NZ)
    x = lax.rem(lax.div(s, NZ), NX)
    y = lax.div(s, NZ * NX)
    base = s - z

    zright = base + lax.rem(z + 1, NZ)
    zleft = base + lax.rem(z + NZ - 1, NZ)
    ring_next = lax.rem(s + NZ, SLABS)
    ring_prev = lax.rem(s + SLABS - NZ, SLABS)
    xflip = s + NZ * (1 - 2 * x)
    gcore = g + 1 - 2 * lax.rem(g, 2)
    gx = lax.rem(g + 2, NHEAD)
    gxc = gx + 1 - 2 * lax.rem(gx, 2)

    def group_dst(d):
        return (lax.rem(y + lax.rem(d, NY), NY) * NX + lax.rem(x + lax.div(d, NY), NX)) * NZ + z

    def group_src(d):
        return lax.rem(y + NY - lax.rem(d, NY), NY) * NX + lax.rem(x + lax.div(d, NY), NX)

    def remote(src, dst, ssem, rsem, slab, head):
        return pltpu.make_async_remote_copy(
            src_ref=src, dst_ref=dst, send_sem=ssem, recv_sem=rsem,
            device_id=(slab, head), device_id_type=MESH)

    loads = []
    for h in range(H):
        cols = slice(h * HD, (h + 1) * HD)
        loads.append(pltpu.make_async_copy(k_hbm.at[:, :, cols], own.at[h, 0], loc.at[2 * h]))
        loads.append(pltpu.make_async_copy(v_hbm.at[:, :, cols], own.at[h, 1], loc.at[2 * h + 1]))
    for c in loads:
        c.start()
    qload = pltpu.make_async_copy(q_hbm, qv, loc.at[6])
    qload.start()

    barrier = pltpu.get_barrier_semaphore()

    def greet(slab, head):
        pl.semaphore_signal(barrier, inc=1, device_id=(slab, head), device_id_type=MESH)

    for slab, head in ((zright, g), (zleft, g), (s, gcore), (s, gx),
                       (xflip, gx), (xflip, gxc)):
        greet(slab, head)

    @pl.loop(1, NG)
    def _(d):
        greet(group_dst(d), g)

    for c in loads:
        c.wait()
    pl.semaphore_wait(barrier, 6 + NG - 1)

    zcopies = {}

    def z_start(h, step):
        def at(off):
            if h == H:
                return xb[off]
            return own.at[h] if off == 0 else zb[off, h]

        for way, sign, target in ((0, -1, zright), (1, 1, zleft)):
            src = at(sign * (step - 1))
            dst = at(NZ // 2 if step == NZ // 2 else sign * step)
            if step == NZ // 2:
                part = slice(way * KT // 2, (way + 1) * KT // 2)
                part = (part,) if h == H else (slice(0, 2), part)
                src, dst = src.at[part], dst.at[part]
            sem = (way, h, step - 1)
            zcopies[sem] = remote(src, dst, zs.at[sem], zr.at[sem], target, g)
            zcopies[sem].start()

    z_start(0, 1)
    xcopy = remote(own.at[HX, KX], xb[0], xs.at[0], xs.at[1], xflip, g)
    xcopy.start()

    pk[...] = jnp.full((2, 8, 128), -1, jnp.int32)
    pk[0, :2, :SLOTS] = fsv[...]
    pk[1, :2, :SLOTS] = ftv[...]

    def req_copy(d):
        return remote(pk, pkr.at[d], rs.at[0], rr.at[0], group_src(d) * NZ + z, g)

    req_all = remote(pkr.at[1:], pkr.at[1:], rs.at[0], rr.at[0], s, gcore)

    @pl.loop(1, NG)
    def _(d):
        req_copy(d).start()

    pkr[0] = pk[...]

    mid = pltpu.make_async_copy(own, near.at[:, :, NT:NT + KT], loc.at[7])
    mid.start()

    def halo_up(h):
        return remote(zb[-1, h].at[:, KT - NT:], near.at[h, :, :NT], hs.at[h], hr.at[h], ring_next, g)

    def halo_down(h):
        return remote(zb[1, h].at[:, :NT], near.at[h, :, NT + KT:], hs.at[h], hr.at[h], ring_prev, g)

    def halo_start(h):
        @pl.when(z == 0)
        def _():
            halo_up(h).start()

        @pl.when(z != 0)
        def _():
            near[h, :, :NT] = zb[-1, h][:, KT - NT:]

        @pl.when(z == NZ - 1)
        def _():
            halo_down(h).start()

        @pl.when(z != NZ - 1)
        def _():
            near[h, :, NT + KT:] = zb[1, h][:, :NT]

    def halo_wait(h, sent):
        for end, copy in ((0, halo_up), (NZ - 1, halo_down)):
            @pl.when(z == end)
            def _():
                (copy(h).wait_send if sent else copy(h).wait_recv)()

    req_all.wait_recv()

    listed = pkr[:, 0]
    tiles = pkr[:, 1]
    lane = lax.broadcasted_iota(jnp.int32, (NG, 8, 128), 2)
    table = jnp.zeros((NG, 8, 128), jnp.int32)
    for n in range(2 * NZ):
        first = base if n < NZ else xflip - z
        hit = jnp.where(listed == first + n % NZ, tiles, 0)
        table = jnp.where(lane == n, jnp.sum(hit, axis=2, keepdims=True), table)
    reqv[...] = table
    tosm = pltpu.make_async_copy(reqv, reqs, loc.at[8])
    tosm.start()
    tosm.wait()

    both = slice(0, 2)
    if_plain = ((1, NG, 0, 0, both),)
    if_first = (
        (NY, NG, 0, 0, slice(1 - KX, 2 - KX)),
        (1, NY, 0, 0, both),
        (NY + 1, NG, NY, 1, slice(KX, KX + 1)),
    )

    def groups(h):
        return enumerate(if_first if h == HX else if_plain)

    def tile_refs(h, step, slot, kvs):
        b = step % (NZ // 2)
        rows = slice(0, 2 * KTILE)
        if b == 0:
            half = 0 if step == 0 else 1
            rows = slice(half * KTILE, (half + 1) * KTILE)
        return send.at[h, b, slot, kvs, :, rows, :], recv.at[h, b, slot, kvs, :, rows, :]

    def tile_copy(h, step, n, slot, d, kvs):
        return remote(*tile_refs(h, step, slot, kvs), ps.at[h, step, n], pr.at[h, step, n], group_dst(d), g)

    def tile_all(h, step):
        return [remote(*tile_refs(h, step, slice(lo, hi), kvs), ps.at[h, step, n], pr.at[h, step, n], s, gcore)
                for n, (lo, hi, _, _, kvs) in groups(h)]

    def pick(h, step, slot, d, other, kvs, dst):
        b = step % (NZ // 2)
        for half, off in ((0, 0),) if step == 0 else (((1, step),) if b == 0 else ((0, step), (1, -step))):
            lane_of = lax.rem(z + (off + NZ), NZ) + NZ * other
            for r in range(2):
                tile = reqs[d, r, lane_of]
                for kv in range(kvs.start, kvs.stop):
                    if other:
                        got = xb[off][tile]
                    else:
                        got = own[h, kv, tile] if off == 0 else zb[off, h][kv, tile]
                    dst[h, b, slot, kv, r, half * KTILE:(half + 1) * KTILE, :] = got

    def select(h, step):
        here = HX if h == H else h
        for n, (lo, hi, back, other, kvs) in groups(here):
            if other != (h == H):
                continue

            @pl.loop(lo, hi)
            def _(slot):
                pick(here, step, slot, slot - back, other, kvs, send)
                tile_copy(here, step, n, slot, slot - back, kvs).start()

        if h == H:
            pick(HX, step, NY, 0, 1, slice(KX, KX + 1), recv)
        else:
            pick(h, step, 0, 0, 0, both, recv)

    for h in range(H):
        select(h, 0)
    xcopy.wait_recv()
    select(H, 0)

    def w_cols(j):
        return w_hbm.at[:, :, pl.ds(pl.multiple_of(j * OUTC, OUTC), OUTC)]

    w_rows = wr.at[:, pl.ds(pl.multiple_of(g * HD, HD), HD), :]
    wown = pltpu.make_async_copy(w_cols(g), w_rows, loc.at[9])
    wown.start()
    wcopies = [
        remote(w_cols(j), w_rows, ws.at[i], wrs.at[i], slab, j)
        for i, (slab, j) in enumerate(((s, gcore), (xflip, gx), (xflip, gxc)))
    ]
    for c in wcopies:
        c.start()

    key = lax.broadcasted_iota(jnp.int32, (8, NG * 2 * KTILE), 1)
    blk = lax.broadcasted_iota(jnp.int32, (8, NG * 2 * KTILE), 0)
    d_of = jnp.where(blk == 0, (key // KTILE) % NG, key // (2 * KTILE))
    half = jnp.where(blk == 0, key // (NG * KTILE), (key // KTILE) % 2)
    off = jnp.where(blk == 0, half * (NZ // 2), jnp.where(half == 0, blk, NZ - blk))
    ring = ((y + NY - d_of % NY) % NY) * NX + (x + d_of // NY) % NX
    slab_of = ring * NZ + (z + off) % NZ
    for r in range(2):
        count = fc[r]

        def mark(j, table):
            return jnp.where((slab_of == fs[r, j]) & (j < count), 0.0, table)

        bias[r] = lax.fori_loop(0, SLOTS, mark, jnp.full((8, NG * 2 * KTILE), NEG, jnp.float32))
    pos = lax.broadcasted_iota(jnp.int32, (1, TOK + 2 * NEAR), 1) + (s * TOK - NEAR)
    nbias[...] = jnp.where((pos >= 0) & (pos < SLABS * TOK), 0.0, NEG)

    def attend(h, i, keys, values, mask, first):
        rows = pl.ds(pl.multiple_of(i * QC, QC), QC)
        scores = lax.dot_general(qv[rows, h * HD:(h + 1) * HD], keys, (((1,), (1,)), ((), ())),
                                 preferred_element_type=jnp.float32)
        scores = scores * SCALE + mask
        top = jnp.max(scores, axis=1, keepdims=True)
        if not first:
            before = mst[h, rows, :1]
            top = jnp.maximum(before, top)
        weights = jnp.exp2(scores - top)
        total = jnp.sum(weights, axis=1, keepdims=True)
        mixed = jnp.dot(weights.astype(jnp.bfloat16), values, preferred_element_type=jnp.float32)
        if not first:
            fade = jnp.exp2(before - top)
            total = total + fade * lst[h, rows, :1]
            mixed = mixed + fade * acc[h, rows, :]
        return rows, top, total, mixed

    def keep(h, rows, top, total, mixed):
        mst[h, rows, :] = jnp.broadcast_to(top, (QC, 128))
        lst[h, rows, :] = jnp.broadcast_to(total, (QC, 128))
        acc[h, rows, :] = mixed

    def attend_near(h):
        if h == 0:
            qload.wait()
            mid.wait()
        halo_wait(h, False)

        @pl.loop(0, TOK // QC)
        def _(i):
            keep(h, *attend(h, i, near[h, 0].reshape(-1, HD), near[h, 1].reshape(-1, HD), nbias[...], True))

    def attend_far(h, step):
        b = step % (NZ // 2)
        for c in tile_all(h, step):
            c.wait_recv()
        half = 0 if step == 0 else 1
        rows = slice(0, 2 * KTILE) if b != 0 else slice(half * KTILE, (half + 1) * KTILE)
        lanes = slice(0, NG * 2 * KTILE) if b != 0 else slice(half * NG * KTILE, (half + 1) * NG * KTILE)

        for part in range(2):
            @pl.loop(part * HALF // QC, (part + 1) * HALF // QC)
            def _(i):
                keys = recv[h, b, :, 0, part, rows].reshape(-1, HD)
                values = recv[h, b, :, 1, part, rows].reshape(-1, HD)
                got = attend(h, i, keys, values, bias[part, b:b + 1, lanes], False)
                if step != NZ // 2:
                    keep(h, *got)
                else:
                    rows_of, _, total, mixed = got
                    att[h, g, rows_of, :] = (mixed / total).astype(jnp.bfloat16)

            if step == NZ // 2:
                share(h, part)

    acopies = {}

    def att_copy(h, part, i, which, head):
        ref = att.at[h, which, part * HALF:(part + 1) * HALF]
        acopies[h, part, i] = remote(ref, ref, ats.at[h, part, i], atr.at[h, part, i], s, head)
        acopies[h, part, i].start()

    def share(h, part):
        att_copy(h, part, 1, g, gx)
        att_copy(h, part, 0, g, gcore)

    def relay(h, part):
        acopies[h, part, 1].wait_recv()
        att_copy(h, part, 2, gx, gcore)

    def project(h, part):
        acopies[h, part, 0].wait_recv()
        acopies[h, part, 2].wait_recv()
        if h == 0 and part == 0:
            wown.wait()
            for c in wcopies:
                c.wait_recv()

        @pl.loop(part * HALF // QC, (part + 1) * HALF // QC)
        def _(i):
            rows = pl.ds(pl.multiple_of(i * QC, QC), QC)
            left = jnp.concatenate([att[h, j, rows, :] for j in range(NHEAD)], axis=1)
            piece = jnp.dot(left, wr[h], preferred_element_type=jnp.float32)
            if h > 0:
                piece = piece + oacc[rows, :]
            if h < H - 1:
                oacc[rows, :] = piece
            else:
                out_ref[rows, :] = piece.astype(jnp.bfloat16)

    items = []
    for h in range(H):
        for step in range(1, NZ // 2 + 1):
            def item(h=h, step=step):
                for what, of in BETWEEN.get((h, step), ()):
                    for part in range(2):
                        (relay if what == 0 else project)(of, part)
                attend_far(h, step)
            items.append(item)

    done = 0
    for n, (h, step) in enumerate(STAGES):
        for sem, c in zcopies.items():
            if sem[1:3] == (h, step - 1):
                c.wait_recv()
        if step == 1 and h < H:
            halo_start(h)
        if step < NZ // 2:
            z_start(h, step + 1)
        for then, what in STARTS:
            if then == (h, step):
                z_start(what, 1)
        select(h, step)
        for h_near, at_stage in enumerate(NEAR_AT):
            if n == at_stage:
                attend_near(h_near)
                attend_far(h_near, 0)
        if n >= LAG:
            items[done]()
            done += 1
    while done < len(items):
        items[done]()
        done += 1
    for part in range(2):
        relay(H - 1, part)
    for part in range(2):
        project(H - 1, part)

    xcopy.wait_send()
    for c in zcopies.values():
        c.wait_send()
    for h in range(H):
        for step in range(NZ // 2 + 1):
            for c in tile_all(h, step):
                c.wait_send()
        halo_wait(h, True)

    req_all.wait_send()

    for c in wcopies + list(acopies.values()):
        c.wait_send()


def body(query_rows, key_rows, value_rows, far_slab, far_tile, far_count, out_weight):
    vm = pltpu.VMEM
    dma = pltpu.SemaphoreType.DMA
    bf = jnp.bfloat16
    f32 = jnp.float32
    any_spec = pl.BlockSpec(memory_space=pl.ANY)
    smem_spec = pl.BlockSpec(memory_space=pltpu.SMEM)
    scratch = [
        vm((H, 2, KT, KTILE, HD), bf),
        vm((H, 2, KT + 2 * NT, KTILE, HD), bf),
        vm((TOK, H * HD), bf),
        vm((H, NZ // 2, NG, 2, 2, 2 * KTILE, HD), bf),
        vm((H, NZ // 2, NG, 2, 2, 2 * KTILE, HD), bf),
        vm((H, NHEAD, TOK, HD), bf),
        vm((H, NHEAD * HD, OUTC), bf),
        vm((TOK, OUTC), f32),
        vm((H, TOK, 128), f32),
        vm((H, TOK, 128), f32),
        vm((H, TOK, HD), f32),
        vm((2, 8, NG * 2 * KTILE), f32),
        vm((1, TOK + 2 * NEAR), f32),
        vm((2, 8, 128), jnp.int32),
        vm((NG, 2, 8, 128), jnp.int32),
        vm((NG, 8, 128), jnp.int32),
        pltpu.SMEM((NG, 8, 128), jnp.int32),
        dma((2, H + 1, NZ // 2)), dma((2, H + 1, NZ // 2)),
        dma((H, NZ // 2 + 1, 3)), dma((H, NZ // 2 + 1, 3)),
        dma((1,)), dma((1,)),
        dma((H,)), dma((H,)),
        dma((3,)), dma((3,)),
        dma((H, 2, 3)), dma((H, 2, 3)),
        dma((2,)),
        dma((10,)),
    ] + [vm((2, KT, KTILE, HD), bf) for _ in range((NZ - 1) * H)]
    scratch += [vm((KT, KTILE, HD), bf) for _ in range(NZ)]
    vmem_spec = pl.BlockSpec(memory_space=pltpu.VMEM)
    call = pl.pallas_call(
        kernel,
        out_shape=jax.ShapeDtypeStruct((TOK, OUTC), bf),
        in_specs=[any_spec, any_spec, any_spec, smem_spec, smem_spec, smem_spec, vmem_spec, vmem_spec, any_spec],
        out_specs=vmem_spec,
        scratch_shapes=scratch,
        compiler_params=pltpu.CompilerParams(
            collective_id=0, has_side_effects=True, vmem_limit_bytes=60 * 1024 * 1024),
        cost_estimate=pl.CostEstimate(
            flops=12_000_000_000, bytes_accessed=8_000_000, transcendentals=18_000_000),
    )
    return call(query_rows, key_rows.reshape(KT, KTILE, H * HD), value_rows.reshape(KT, KTILE, H * HD), far_slab, far_tile, far_count,
                far_slab, far_tile,
                out_weight.reshape(H, HD, NHEAD * OUTC))


def solution(mesh):
    return jax.shard_map(
        body,
        mesh=mesh,
        in_specs=(
            P("slab", "head"),
            P("slab", "head"),
            P("slab", "head"),
            P("slab", None),
            P("slab", None),
            P("slab"),
            P("head", None),
        ),
        out_specs=P("slab", "head"),
        check_vma=False,
    )
```
